128 devices in a mesh: ia: 16 (over x, z), ja: 4 (over y), ka: 2 (over core).
Axes of the slice: x: 4, y: 4, z: 4, core: 2. Of those that a mesh axis runs over, the one named last changes fastest.
Arguments:
- tensor: float32 [1024, 1024, 512], P('ia', 'ja', 'ka'), may hold values from -6 to 6
- factor_first: float32 [1024, 32], P(('ia', 'ja', 'ka')), may hold values from -0.75 to 0.75
- factor_second: float32 [1024, 32], P(('ja', 'ia', 'ka')), may hold values from -0.375 to 0.375
- factor_third: float32 [512, 32], P(('ka', 'ia', 'ja')), may hold values from -0.375 to 0.375
Outputs:
- gradient: float32 [1024, 32], P(('ia', 'ja', 'ka'))
The draws below stay inside these ranges and needn't reach their ends.
All inputs are finite; a program needn't handle non-finite values.
Results may differ from the reference program's by a relative error of at most 0.000082.
Values sent between devices are 32-bit elements; how exact they have to be, the bound alone decides.
No kernel may reach another device: no remote copies, remote signals or barrier semaphores. Data moves between devices by JAX's collectives and lax.ppermute only.
A program may use at most 64 MiB of HBM per device.

```python
import jax
import jax.numpy as jnp
from jax import lax

I = 1024
J = 1024
K = 512
R = 32


def strengthened(result, stream_key, source, target, shards_of, factor):
    owner, partner = [(jnp.arange(result.shape[axis_at]) // (result.shape[axis_at] // shards_of)).reshape([-1 if axis == axis_at else 1 for axis in range(result.ndim)]) for axis_at in (source, target)]
    chosen = jax.random.permutation(stream_key, shards_of)[partner]
    strong = (owner == chosen) | (owner == (partner + shards_of // 2) % shards_of)
    return jnp.where(strong, factor * result, result)


def block_scale(stream_key, extent, cuts, least, top_value):
    factor_of = 1.0
    for position, parts in cuts:
        heights = jax.random.uniform(jax.random.fold_in(jax.random.fold_in(stream_key, 6), position), (parts,), jnp.float32, least / len(cuts), top_value / len(cuts))
        factor_of = factor_of * jnp.repeat(jnp.exp(heights), extent[position] // parts).reshape((-1,) + (1,) * (len(extent) - 1 - position))
    return factor_of


def normal_values(stream_key, shape, deviation, limit, split=(), dtype=jnp.bfloat16):
    drawn = jax.random.normal(stream_key, shape, jnp.float32) * deviation
    if len(split) > 0:
        drawn = block_scale(stream_key, shape, split, -0.22, 0.18) * drawn
    return jnp.clip(drawn, min=-limit, max=limit).astype(dtype)


def noise_with(own_key, shape, deviation, bound, pieces, heavy, kind=jnp.bfloat16):
    drawn = deviation * jax.random.normal(own_key, shape, jnp.float32)
    if pieces:
        drawn = drawn * block_scale(own_key, shape, pieces, -0.22, 0.18)
    return jnp.clip(strengthened(drawn, jax.random.fold_in(own_key, 3), *heavy), -bound, bound).astype(kind)


def setup_inputs(seed: int = 0) -> dict:
    seeds = jax.random.split(jax.random.key(seed), 5)
    return {
        "tensor": noise_with(seeds[0], (I, J, K), 1.0, 6.0, ((0, 16), (1, 4), (2, 2)), (1, 0, 16, 2.0), jnp.float32),
        "factor_first": normal_values(seeds[1], (I, R), 0.125, 0.75, ((0, 128),), jnp.float32),
        "factor_second": normal_values(seeds[2], (J, R), 0.0625, 0.375, ((0, 128),), jnp.float32),
        "factor_third": normal_values(seeds[3], (K, R), 0.0625, 0.375, ((0, 128),), jnp.float32),
    }


def reference(tensor, factor_first, factor_second, factor_third):
    blocks = tensor.reshape(I // 64, 64, J, K)

    def one_block(block):
        partial_value = jnp.einsum("ijk,kr->ijr", block, factor_third, precision=lax.Precision.HIGHEST)
        return jnp.einsum("ijr,jr->ir", partial_value, factor_second, precision=lax.Precision.HIGHEST)

    product = lax.map(one_block, blocks).reshape(I, R)
    gram_second = jnp.dot(factor_second.T, factor_second, precision=lax.Precision.HIGHEST)
    gram_third = jnp.dot(factor_third.T, factor_third, precision=lax.Precision.HIGHEST)
    return jnp.dot(factor_first, gram_second * gram_third, precision=lax.Precision.HIGHEST) - product
```

```python
import functools

import jax
import jax.numpy as jnp
from jax import lax
from jax.experimental import pallas as pl
from jax.experimental.pallas import tpu as pltpu
from jax.sharding import PartitionSpec as P

RANK = 32
EVERY = ("ia", "ja", "ka")
HIGHEST = lax.Precision.HIGHEST


def iota(shape, axis):
    return lax.broadcasted_iota(jnp.int32, shape, axis)


def split(value):
    high = value.astype(jnp.bfloat16)
    low = (value - high.astype(jnp.float32)).astype(jnp.bfloat16)
    return high, low


def mm(left, right):
    return jnp.dot(left, right, preferred_element_type=jnp.float32)


def unpacked(packed, rows, source, place):
    count, lanes = packed.shape
    pick = jnp.where(iota((rows, count), 1) == source, 1.0, 0.0).astype(jnp.bfloat16)
    keep = iota((rows, lanes), 1) // RANK == place
    parts = []
    for part in split(packed):
        parts.append(jnp.where(keep, mm(pick, part), 0.0).astype(jnp.bfloat16))
    return parts


def folding(lanes, columns, shift):
    row, column = iota((lanes, columns), 0), iota((lanes, columns), 1)
    hit = (column - shift == row % RANK) & (column >= shift) & (column < shift + RANK)
    return jnp.where(hit, 1.0, 0.0).astype(jnp.bfloat16)


def term_kernel(steps, tensor_ref, packed_ref, term_ref, weight_ref, second_ref, sums_ref):
    ja, ka = lax.axis_index("ja"), lax.axis_index("ka")
    rows, js, ks = tensor_ref.shape
    wide = 4 * RANK

    third_at = iota((ks, 1), 0)
    high, low = unpacked(packed_ref[:, 256:384], ks, third_at // 4 * 2 + ka, third_at % 4)
    weight = mm(high, folding(wide, wide, 0)) + mm(low, folding(wide, wide, RANK))
    weight_ref[...] = weight.astype(jnp.bfloat16)

    second_at = iota((js, 1), 0)
    high, low = unpacked(packed_ref[:, 0:256], js, second_at // 16 * 8 + 2 * ja + second_at // 8 % 2, second_at % 8)
    both = folding(2 * wide, wide, 0) + folding(2 * wide, wide, RANK)
    second_ref[...] = mm(high, both) + mm(low, both)

    per = rows // steps

    def step(at, carry):
        block = tensor_ref[pl.ds(at * per, per)].reshape(per * js, ks)
        high, low = split(block)
        partial = mm(high, weight_ref[...]) + mm(low, weight_ref[...])
        scaled = partial.reshape(per, js, wide) * second_ref[...][None]
        sums_ref[pl.ds(at * per, per)] = jnp.sum(scaled.reshape(per, js // 8, 8, wide), axis=1)
        return carry

    lax.fori_loop(0, steps, step, 0)
    total = jnp.sum(sums_ref[...], axis=1)
    term_ref[...] = total[:, 0:RANK] + total[:, RANK : 2 * RANK]


def gradient_kernel(packed_ref, first_ref, terms_ref, gradient_ref):
    def gram(block):
        lanes = block.shape[1]
        whole = lax.dot_general(block, block, (((0,), (0,)), ((), ())), precision=HIGHEST)
        kept = jnp.where(iota((lanes, lanes), 0) // RANK == iota((lanes, lanes), 1) // RANK, whole, 0.0)
        fold = jnp.where(iota((lanes, RANK), 0) % RANK == iota((lanes, RANK), 1), 1.0, 0.0)
        tall = jnp.dot(kept, fold, precision=HIGHEST)
        return jnp.sum(tall.reshape(lanes // RANK, RANK, RANK), axis=0)

    both = gram(packed_ref[:, 0:256]) * gram(packed_ref[:, 256:384])
    rows = first_ref.shape[0]
    product = jnp.sum(terms_ref[...].reshape(-1, rows, RANK), axis=0)
    gradient_ref[...] = jnp.dot(first_ref[...], both, precision=HIGHEST) - product


def on_device(tensor, first, second, third):
    rows, js, ks = tensor.shape
    own = jnp.concatenate([second.reshape(1, 256), third.reshape(1, 128)], axis=1)
    packed = lax.all_to_all(jnp.broadcast_to(own, (128, 384)), EVERY, 0, 0, tiled=True)
    tensor = pltpu.with_memory_space_constraint(tensor, pltpu.VMEM)
    term = pl.pallas_call(
        functools.partial(term_kernel, 16),
        out_shape=jax.ShapeDtypeStruct((rows, RANK), jnp.float32),
        in_specs=[pl.BlockSpec(memory_space=pltpu.VMEM)] * 2,
        out_specs=pl.BlockSpec(memory_space=pltpu.VMEM),
        scratch_shapes=[
            pltpu.VMEM((ks, 4 * RANK), jnp.bfloat16),
            pltpu.VMEM((js, 4 * RANK), jnp.float32),
            pltpu.VMEM((rows, 8, 4 * RANK), jnp.float32),
        ],
        compiler_params=pltpu.CompilerParams(vmem_limit_bytes=24 * 1024 * 1024),
        cost_estimate=pl.CostEstimate(flops=2 * rows * js * ks * 512, bytes_accessed=rows * js * ks * 4, transcendentals=0),
        name="term",
    )(tensor, packed)
    terms = lax.all_to_all(term, ("ja", "ka"), 0, 0, tiled=True)
    return pl.pallas_call(
        gradient_kernel,
        out_shape=jax.ShapeDtypeStruct(first.shape, jnp.float32),
        in_specs=[pl.BlockSpec(memory_space=pltpu.VMEM)] * 3,
        out_specs=pl.BlockSpec(memory_space=pltpu.VMEM),
        compiler_params=pltpu.CompilerParams(vmem_limit_bytes=16 * 1024 * 1024),
        name="gradient",
    )(packed, first, terms)


def solution(mesh):
    return jax.shard_map(
        on_device,
        mesh=mesh,
        in_specs=(
            P("ia", "ja", "ka"),
            P(("ia", "ja", "ka"), None),
            P(("ja", "ia", "ka"), None),
            P(("ka", "ia", "ja"), None),
        ),
        out_specs=P(("ia", "ja", "ka"), None),
        check_vma=False,
    )
```

```python
import functools

import jax
import jax.numpy as jnp
from jax import lax
from jax.experimental import pallas as pl
from jax.experimental.pallas import tpu as pltpu
from jax.sharding import PartitionSpec as P

RANK = 32
EVERY = ("ia", "ja", "ka")
CHUNK = 4
CHUNKS = 16
GROUP = 4
AHEAD = 8
PER_HOP = 2
HIGHEST = lax.Precision.HIGHEST


def iota(shape, axis):
    return lax.broadcasted_iota(jnp.int32, shape, axis)


def split(value):
    high = value.astype(jnp.bfloat16)
    low = (value - high.astype(jnp.float32)).astype(jnp.bfloat16)
    return high, low


def chunks_ahead():
    ia, ja = lax.axis_index("ia"), lax.axis_index("ja")
    hops = sum(jnp.minimum(at, 4 - at) for at in (ia // 4, ia % 4, ja))
    return jnp.clip(AHEAD - PER_HOP * hops, 0, CHUNKS)


def chunk_copy(tensor_hbm, tensor_ref, sem, at):
    here = pl.ds(at * CHUNK, CHUNK)
    return pltpu.make_async_copy(tensor_hbm.at[here], tensor_ref.at[here], sem)


def own_kernel(second_hbm, third_hbm, tensor_hbm, own_ref, tensor_ref, second_ref, third_ref, sems):
    second_copy = pltpu.make_async_copy(second_hbm, second_ref, sems.at[0])
    third_copy = pltpu.make_async_copy(third_hbm, third_ref, sems.at[1])
    second_copy.start()
    third_copy.start()
    ahead = chunks_ahead()

    @pl.loop(0, ahead)
    def begin(at):
        chunk_copy(tensor_hbm, tensor_ref, sems.at[2 + at], at).start()

    def row(value):
        count = value.shape[0]
        lanes = count * RANK
        spread = jnp.where(iota((RANK, lanes), 0) == iota((RANK, lanes), 1) % RANK, 1.0, 0.0)
        wide = jnp.dot(value, spread, precision=HIGHEST)
        kept = jnp.where(iota((count, lanes), 1) // RANK == iota((count, lanes), 0), wide, 0.0)
        return jnp.sum(kept, axis=0, keepdims=True)

    second_copy.wait()
    third_copy.wait()
    own = jnp.concatenate([row(second_ref[...]), row(third_ref[...])], axis=1)
    own_ref[...] = jnp.broadcast_to(own[None], own_ref.shape)

    @pl.loop(0, ahead)
    def end(at):
        chunk_copy(tensor_hbm, tensor_ref, sems.at[2 + at], at).wait()


def term_kernel(tensor_hbm, packed_ref, held_ref, term_ref, tensor_ref, third_ref, second_ref, sums_ref, sems):
    del held_ref
    ahead = chunks_ahead()

    @pl.loop(ahead, CHUNKS)
    def begin(at):
        chunk_copy(tensor_hbm, tensor_ref, sems.at[at], at).start()

    def arrive(at):
        @pl.when(at >= ahead)
        def wait():
            chunk_copy(tensor_hbm, tensor_ref, sems.at[at], at).wait()

    rows, js, ks = tensor_ref.shape
    wide = 4 * RANK
    ja, ka = lax.axis_index("ja"), lax.axis_index("ka")

    def spread(source, into, start, stride):
        count = source.shape[0]
        for part in range(4):
            turned = pltpu.roll(source, (wide - RANK * part) % wide, 1)
            into[pl.ds(start + part, count, stride=stride), :] = turned

    spread(packed_ref[pl.ds(3 * ka + 2, ks // 4, stride=6), :], third_ref, 0, 4)
    for core in range(2):
        for half in range(2):
            source = packed_ref[pl.ds(6 * ja + 3 * core + half, js // 16, stride=24), :]
            spread(source, second_ref, 8 * core + 4 * half, 16)
    lane = iota((ks, wide), 1)
    high, low = split(third_ref[...])
    turned = pltpu.roll(low.astype(jnp.float32), RANK, 1)
    weight = jnp.where(lane < RANK, high.astype(jnp.float32), jnp.where(lane < 2 * RANK, turned, 0.0)).astype(jnp.bfloat16)
    weight = jnp.concatenate([weight, jnp.zeros_like(weight)], axis=1)
    second = second_ref[...]
    second_ref[...] = jnp.where(lane < RANK, second, pltpu.roll(second, RANK, 1))

    def contract(*sums):
        for unit in range(2):
            pltpu.matmul_push_rhs(weight, 0, unit)
        for unit in range(2):
            pltpu.matmul_acc_lhs(sums[unit], jnp.zeros((js, ks), jnp.bfloat16), load_staged_rhs=0)
            pltpu.matmul_pop(sums[unit])
        lag = len(sums) - 1

        def push(at, turn):
            high, low = split(tensor_ref[at])
            pltpu.matmul_acc_lhs(sums[turn % len(sums)], high)
            pltpu.matmul_acc_lhs(sums[turn % len(sums)], low)

        def pop(at, turn):
            scaled = pltpu.matmul_pop(sums[turn % len(sums)])[:, 0:wide] * second_ref[...]
            sums_ref[at] = jnp.sum(scaled.reshape(js // 8, 8, wide), axis=0)

        arrive(0)
        for step in range(lag):
            push(step, step)

        per = GROUP // CHUNK

        @pl.loop(0, rows // GROUP - 1)
        def block(group):
            for chunk in range(per):
                arrive(group * per + 1 + chunk)
            for step in range(GROUP):
                push(group * GROUP + lag + step, lag + step)
                pop(group * GROUP + step, step)

        for chunk in range(CHUNKS - per + 1, CHUNKS):
            arrive(chunk)
        for at in range(rows - GROUP, rows):
            if at + lag < rows:
                push(at + lag, at + lag)
            pop(at, at)

    pl.run_scoped(contract, *[pltpu.ACC(at % 2)((js, 256), jnp.float32) for at in range(4)])
    term_ref[...] = jnp.sum(sums_ref[...], axis=1).reshape(term_ref.shape)


def gram_kernel(packed_ref, first_ref, gram_ref):
    packed = packed_ref[...].reshape(128, 384)

    def gram(block):
        lanes = block.shape[1]
        whole = lax.dot_general(block, block, (((0,), (0,)), ((), ())), precision=HIGHEST)
        kept = jnp.where(iota((lanes, lanes), 0) // RANK == iota((lanes, lanes), 1) // RANK, whole, 0.0)
        fold = jnp.where(iota((lanes, RANK), 0) % RANK == iota((lanes, RANK), 1), 1.0, 0.0)
        tall = jnp.dot(kept, fold, precision=HIGHEST)
        return jnp.sum(tall.reshape(lanes // RANK, RANK, RANK), axis=0)

    both = gram(packed[:, 0:256]) * gram(packed[:, 256:384])
    gram_ref[...] = jnp.dot(first_ref[...], both, precision=HIGHEST)


def gradient_kernel(gram_ref, terms_ref, gradient_ref):
    total = jnp.sum(terms_ref[...], axis=0)
    gradient_ref[...] = gram_ref[...] - (total[:, 0:RANK] + total[:, RANK : 2 * RANK])


def fixed(value):
    return pltpu.with_memory_space_constraint(value, pltpu.VMEM)


def inhbm(value):
    return pltpu.with_memory_space_constraint(value, pltpu.HBM)


VMEM = pl.BlockSpec(memory_space=pltpu.VMEM)


def on_device(tensor, first, second, third):
    rows, js, ks = tensor.shape
    tensor = inhbm(tensor)
    own, held = pl.pallas_call(
        own_kernel,
        out_shape=(jax.ShapeDtypeStruct((128, 1, 384), jnp.float32), jax.ShapeDtypeStruct(tensor.shape, jnp.float32)),
        in_specs=[pl.BlockSpec(memory_space=pltpu.HBM)] * 3,
        out_specs=(VMEM, VMEM),
        scratch_shapes=[pltpu.VMEM((8, RANK), jnp.float32), pltpu.VMEM((4, RANK), jnp.float32), pltpu.SemaphoreType.DMA((2 + CHUNKS,))],
        compiler_params=pltpu.CompilerParams(vmem_limit_bytes=24 * 1024 * 1024),
        name="own",
    )(inhbm(second), inhbm(third), tensor)
    packed = lax.all_to_all(own, EVERY, 0, 0, tiled=True)
    term, _ = pl.pallas_call(
        term_kernel,
        out_shape=(jax.ShapeDtypeStruct((8, 8, 4 * RANK), jnp.float32), jax.ShapeDtypeStruct(tensor.shape, jnp.float32)),
        in_specs=[pl.BlockSpec(memory_space=pltpu.HBM), VMEM, VMEM],
        out_specs=(VMEM, VMEM),
        input_output_aliases={2: 1},
        scratch_shapes=[
            pltpu.VMEM((ks, 4 * RANK), jnp.float32),
            pltpu.VMEM((js, 4 * RANK), jnp.float32),
            pltpu.VMEM((rows, 8, 4 * RANK), jnp.float32),
            pltpu.SemaphoreType.DMA((CHUNKS,)),
        ],
        compiler_params=pltpu.CompilerParams(vmem_limit_bytes=24 * 1024 * 1024),
        cost_estimate=pl.CostEstimate(flops=2 * rows * js * ks * 512, bytes_accessed=rows * js * ks * 4, transcendentals=0),
        name="term",
    )(tensor, packed.reshape(384, 128), held)
    terms = lax.all_to_all(term, ("ja", "ka"), 0, 0, tiled=True)
    gram = pl.pallas_call(
        gram_kernel,
        out_shape=jax.ShapeDtypeStruct(first.shape, jnp.float32),
        in_specs=[VMEM] * 2,
        out_specs=VMEM,
        compiler_params=pltpu.CompilerParams(vmem_limit_bytes=16 * 1024 * 1024),
        cost_estimate=pl.CostEstimate(flops=1 << 27, bytes_accessed=1 << 20, transcendentals=0),
        name="gram",
    )(packed, first)
    return pl.pallas_call(
        gradient_kernel,
        out_shape=jax.ShapeDtypeStruct(first.shape, jnp.float32),
        in_specs=[VMEM] * 2,
        out_specs=VMEM,
        compiler_params=pltpu.CompilerParams(vmem_limit_bytes=4 * 1024 * 1024),
        name="gradient",
    )(gram, terms)


def solution(mesh):
    return jax.shard_map(
        on_device,
        mesh=mesh,
        in_specs=(
            P("ia", "ja", "ka"),
            P(("ia", "ja", "ka"), None),
            P(("ja", "ia", "ka"), None),
            P(("ka", "ia", "ja"), None),
        ),
        out_specs=P(("ia", "ja", "ka"), None),
        check_vma=False,
    )
```

```python
import functools

import jax
import jax.numpy as jnp
from jax import lax
from jax.experimental import pallas as pl
from jax.experimental.pallas import tpu as pltpu
from jax.sharding import PartitionSpec as P

RANK = 32
EVERY = ("ia", "ja", "ka")
CHUNK = 4
CHUNKS = 16
GROUP = 8
AHEAD = 12
PER_HOP = 6
PER_ROW = 0
HIGHEST = lax.Precision.HIGHEST


def iota(shape, axis):
    return lax.broadcasted_iota(jnp.int32, shape, axis)


def split(value):
    high = value.astype(jnp.bfloat16)
    low = (value - high.astype(jnp.float32)).astype(jnp.bfloat16)
    return high, low


def chunks_ahead():
    ia, ja = lax.axis_index("ia"), lax.axis_index("ja")
    near = sum(jnp.minimum(at, 4 - at) for at in (ia // 4, ia % 4))
    return jnp.clip(AHEAD - PER_HOP * near - PER_ROW * jnp.minimum(ja, 4 - ja), 0, CHUNKS)


def chunk_copy(tensor_hbm, tensor_ref, sem, at):
    here = pl.ds(at * CHUNK, CHUNK)
    return pltpu.make_async_copy(tensor_hbm.at[here], tensor_ref.at[here], sem)


def own_kernel(second_hbm, third_hbm, tensor_hbm, own_ref, tensor_ref, second_ref, third_ref, sems):
    second_copy = pltpu.make_async_copy(second_hbm, second_ref, sems.at[0])
    third_copy = pltpu.make_async_copy(third_hbm, third_ref, sems.at[1])
    second_copy.start()
    third_copy.start()
    ahead = chunks_ahead()

    @pl.loop(0, ahead)
    def begin(at):
        chunk_copy(tensor_hbm, tensor_ref, sems.at[2 + at], at).start()

    def row(value):
        count = value.shape[0]
        lanes = count * RANK
        spread = jnp.where(iota((RANK, lanes), 0) == iota((RANK, lanes), 1) % RANK, 1.0, 0.0)
        wide = jnp.dot(value, spread, precision=HIGHEST)
        kept = jnp.where(iota((count, lanes), 1) // RANK == iota((count, lanes), 0), wide, 0.0)
        return jnp.sum(kept, axis=0, keepdims=True)

    second_copy.wait()
    third_copy.wait()
    own = jnp.concatenate([row(second_ref[...]), row(third_ref[...])], axis=1)
    own_ref[...] = jnp.broadcast_to(own[None], own_ref.shape)

    @pl.loop(0, ahead)
    def end(at):
        chunk_copy(tensor_hbm, tensor_ref, sems.at[2 + at], at).wait()


def term_kernel(tensor_hbm, packed_ref, held_ref, term_ref, tensor_ref, third_ref, second_ref, lines_ref, sums_ref, sems):
    del held_ref
    ahead = chunks_ahead()

    @pl.loop(ahead, CHUNKS)
    def begin(at):
        chunk_copy(tensor_hbm, tensor_ref, sems.at[at], at).start()

    def arrive(at):
        @pl.when(at >= ahead)
        def wait():
            chunk_copy(tensor_hbm, tensor_ref, sems.at[at], at).wait()

    rows, js, ks = tensor_ref.shape
    wide = 4 * RANK
    ja, ka = lax.axis_index("ja"), lax.axis_index("ka")

    def spread(source, into, start, stride):
        count = source.shape[0]
        for part in range(4):
            turned = pltpu.roll(source, (wide - RANK * part) % wide, 1)
            into[pl.ds(start + part, count, stride=stride), :] = turned

    spread(packed_ref[pl.ds(3 * ka + 2, ks // 4, stride=6), :], third_ref, 0, 4)
    for core in range(2):
        for half in range(2):
            source = packed_ref[pl.ds(6 * ja + 3 * core + half, js // 16, stride=24), :]
            spread(source, second_ref, 8 * core + 4 * half, 16)
    both = jnp.where(iota((js, wide), 1) < RANK, second_ref[...], pltpu.roll(third_ref[...], RANK, 1)).T
    high, low = split(both[0:RANK])
    left = jnp.concatenate([high, low], axis=0)
    lines_ref[...] = jnp.concatenate([both[RANK : 2 * RANK]] * 2, axis=0)

    def contract(*sums):
        lag = len(sums) - 1

        def push(at, turn):
            into = sums[turn % len(sums)]
            for register, part in enumerate(split(tensor_ref[at])):
                pltpu.matmul_push_rhs(part, register, turn % 2)
                pltpu.matmul_acc_lhs(into, left, load_staged_rhs=register)

        def pop(at, turn):
            scaled = pltpu.matmul_pop(sums[turn % len(sums)]) * lines_ref[...]
            scaled = scaled[:, 0:wide] + scaled[:, wide : 2 * wide]
            sums_ref[at] = scaled[0:RANK] + scaled[RANK : 2 * RANK]

        arrive(0)
        for step in range(lag):
            push(step, step)

        per = GROUP // CHUNK
        free = jnp.minimum(jnp.maximum(ahead - 1, 0) // per, rows // GROUP - 1)

        def contract_group(group):
            for step in range(GROUP):
                push(group * GROUP + lag + step, lag + step)
                pop(group * GROUP + step, step)

        pl.loop(0, free)(contract_group)

        @pl.loop(free, rows // GROUP - 1)
        def block(group):
            for chunk in range(per):
                arrive(group * per + chunk + 1)
            contract_group(group)

        for chunk in range(CHUNKS - GROUP // CHUNK + 1, CHUNKS):
            arrive(chunk)
        for at in range(rows - GROUP, rows):
            if at + lag < rows:
                push(at + lag, at + lag)
            pop(at, at)

    pl.run_scoped(contract, *[pltpu.ACC(at % 2)((2 * RANK, 256), jnp.float32) for at in range(4)])
    term_ref[...] = jnp.zeros_like(term_ref)
    term_ref[:, :, 0:RANK] = jnp.sum(sums_ref[...].reshape(8, 8, RANK, wide), axis=3)


def gradient_kernel(packed_ref, first_ref, terms_ref, gradient_ref):
    packed = packed_ref[...]
    is_third = iota(packed.shape, 0) % 3 == 2

    def gram(block):
        parts = jnp.concatenate(split(block), axis=1)
        whole = lax.dot_general(parts, parts, (((0,), (0,)), ((), ())), preferred_element_type=jnp.float32)
        wide = block.shape[1]
        whole = whole[0:wide] + whole[wide : 2 * wide]
        whole = whole[:, 0:wide] + whole[:, wide : 2 * wide]
        spans = [slice(at, at + RANK) for at in range(0, wide, RANK)]
        return sum(whole[span, span] for span in spans)

    both = gram(jnp.where(is_third, 0.0, packed)) * gram(jnp.where(is_third, packed, 0.0))
    product = jnp.sum(terms_ref[:, :, 0:RANK], axis=0)
    gradient_ref[...] = jnp.dot(first_ref[...], both, precision=HIGHEST) - product


def inhbm(value):
    return pltpu.with_memory_space_constraint(value, pltpu.HBM)


VMEM = pl.BlockSpec(memory_space=pltpu.VMEM)


def on_device(tensor, first, second, third):
    rows, js, ks = tensor.shape
    tensor = inhbm(tensor)
    own, held = pl.pallas_call(
        own_kernel,
        out_shape=(jax.ShapeDtypeStruct((128, 1, 384), jnp.float32), jax.ShapeDtypeStruct(tensor.shape, jnp.float32)),
        in_specs=[pl.BlockSpec(memory_space=pltpu.HBM)] * 3,
        out_specs=(VMEM, VMEM),
        scratch_shapes=[pltpu.VMEM((8, RANK), jnp.float32), pltpu.VMEM((4, RANK), jnp.float32), pltpu.SemaphoreType.DMA((2 + CHUNKS,))],
        compiler_params=pltpu.CompilerParams(vmem_limit_bytes=24 * 1024 * 1024),
        name="own",
    )(inhbm(second), inhbm(third), tensor)
    packed = lax.all_to_all(own, EVERY, 0, 0, tiled=True).reshape(384, 128)
    term, _ = pl.pallas_call(
        term_kernel,
        out_shape=(jax.ShapeDtypeStruct((8, 8, 4 * RANK), jnp.float32), jax.ShapeDtypeStruct(tensor.shape, jnp.float32)),
        in_specs=[pl.BlockSpec(memory_space=pltpu.HBM), VMEM, VMEM],
        out_specs=(VMEM, VMEM),
        input_output_aliases={2: 1},
        scratch_shapes=[
            pltpu.VMEM((ks, 4 * RANK), jnp.float32),
            pltpu.VMEM((js, 4 * RANK), jnp.float32),
            pltpu.VMEM((2 * RANK, ks), jnp.float32),
            pltpu.VMEM((rows, RANK, 4 * RANK), jnp.float32),
            pltpu.SemaphoreType.DMA((CHUNKS,)),
        ],
        compiler_params=pltpu.CompilerParams(vmem_limit_bytes=24 * 1024 * 1024),
        cost_estimate=pl.CostEstimate(flops=2 * rows * js * ks * 512, bytes_accessed=rows * js * ks * 4, transcendentals=0),
        name="term",
    )(tensor, packed, held)
    terms = lax.all_to_all(term, ("ja", "ka"), 0, 0, tiled=True)
    return pl.pallas_call(
        gradient_kernel,
        out_shape=jax.ShapeDtypeStruct(first.shape, jnp.float32),
        in_specs=[VMEM] * 3,
        out_specs=VMEM,
        compiler_params=pltpu.CompilerParams(vmem_limit_bytes=8 * 1024 * 1024),
        name="gradient",
    )(packed, first, terms)


def solution(mesh):
    return jax.shard_map(
        on_device,
        mesh=mesh,
        in_specs=(
            P("ia", "ja", "ka"),
            P(("ia", "ja", "ka"), None),
            P(("ja", "ia", "ka"), None),
            P(("ka", "ia", "ja"), None),
        ),
        out_specs=P(("ia", "ja", "ka"), None),
        check_vma=False,
    )
```

```python
import functools

import jax
import jax.numpy as jnp
from jax import lax
from jax.experimental import pallas as pl
from jax.experimental.pallas import tpu as pltpu
from jax.sharding import PartitionSpec as P

RANK = 32
EVERY = ("ia", "ja", "ka")
CHUNK = 4
CHUNKS = 16
GROUP = 8
AHEAD = 12
PER_HOP = 6
PER_ROW = 0
HIGHEST = lax.Precision.HIGHEST


def iota(shape, axis):
    return lax.broadcasted_iota(jnp.int32, shape, axis)


def split(value):
    high = value.astype(jnp.bfloat16)
    low = (value - high.astype(jnp.float32)).astype(jnp.bfloat16)
    return high, low


def chunks_ahead():
    ia, ja = lax.axis_index("ia"), lax.axis_index("ja")
    near = sum(jnp.minimum(at, 4 - at) for at in (ia // 4, ia % 4))
    return jnp.clip(AHEAD - PER_HOP * near - PER_ROW * jnp.minimum(ja, 4 - ja), 0, CHUNKS)


def chunk_copy(tensor_hbm, tensor_ref, sem, at):
    here = pl.ds(at * CHUNK, CHUNK)
    return pltpu.make_async_copy(tensor_hbm.at[here], tensor_ref.at[here], sem)


def own_kernel(second_hbm, third_hbm, tensor_hbm, own_ref, tensor_ref, second_ref, third_ref, sems):
    second_copy = pltpu.make_async_copy(second_hbm, second_ref, sems.at[0])
    third_copy = pltpu.make_async_copy(third_hbm, third_ref, sems.at[1])
    second_copy.start()
    third_copy.start()
    ahead = chunks_ahead()

    @pl.loop(0, ahead)
    def begin(at):
        chunk_copy(tensor_hbm, tensor_ref, sems.at[2 + at], at).start()

    def row(value):
        return jnp.concatenate([value[at : at + 1] for at in range(value.shape[0])], axis=1)

    second_copy.wait()
    third_copy.wait()
    own = jnp.concatenate([row(second_ref[...]), row(third_ref[...])], axis=1)
    own_ref[...] = jnp.broadcast_to(own[None], own_ref.shape)

    @pl.loop(0, ahead)
    def end(at):
        chunk_copy(tensor_hbm, tensor_ref, sems.at[2 + at], at).wait()


def term_kernel(tensor_hbm, packed_ref, held_ref, term_ref, tensor_ref, third_ref, second_ref, lines_ref, sums_ref, sems):
    del held_ref
    ahead = chunks_ahead()

    @pl.loop(ahead, CHUNKS)
    def begin(at):
        chunk_copy(tensor_hbm, tensor_ref, sems.at[at], at).start()

    def arrive(at):
        @pl.when(at >= ahead)
        def wait():
            chunk_copy(tensor_hbm, tensor_ref, sems.at[at], at).wait()

    rows, js, ks = tensor_ref.shape
    wide = 4 * RANK
    ja, ka = lax.axis_index("ja"), lax.axis_index("ka")

    def spread(source, into, start, stride):
        count = source.shape[0]
        for part in range(4):
            turned = pltpu.roll(source, (wide - RANK * part) % wide, 1)
            into[pl.ds(start + part, count, stride=stride), :] = turned

    spread(packed_ref[pl.ds(3 * ka + 2, ks // 4, stride=6), :], third_ref, 0, 4)
    for core in range(2):
        for half in range(2):
            source = packed_ref[pl.ds(6 * ja + 3 * core + half, js // 16, stride=24), :]
            spread(source, second_ref, 8 * core + 4 * half, 16)
    both = jnp.where(iota((js, wide), 1) < RANK, second_ref[...], pltpu.roll(third_ref[...], RANK, 1)).T
    high, low = split(both[0:RANK])
    left = jnp.concatenate([high, low], axis=0)
    lines_ref[...] = jnp.concatenate([both[RANK : 2 * RANK]] * 2, axis=0)

    def contract(*sums):
        lag = len(sums) - 1

        def push(at, turn):
            into = sums[turn % len(sums)]
            for register, part in enumerate(split(tensor_ref[at])):
                pltpu.matmul_push_rhs(part, register, turn % 2)
                pltpu.matmul_acc_lhs(into, left, load_staged_rhs=register)

        def pop(at, turn):
            scaled = pltpu.matmul_pop(sums[turn % len(sums)]) * lines_ref[...]
            scaled = scaled[:, 0:wide] + scaled[:, wide : 2 * wide]
            sums_ref[at] = scaled[0:RANK] + scaled[RANK : 2 * RANK]

        arrive(0)
        for step in range(lag):
            push(step, step)

        per = GROUP // CHUNK
        free = jnp.minimum(jnp.maximum(ahead - 1, 0) // per, rows // GROUP - 1)

        def contract_group(group):
            for step in range(GROUP):
                push(group * GROUP + lag + step, lag + step)
                pop(group * GROUP + step, step)

        pl.loop(0, free)(contract_group)

        @pl.loop(free, rows // GROUP - 1)
        def block(group):
            for chunk in range(per):
                arrive(group * per + chunk + 1)
            contract_group(group)

        for chunk in range(CHUNKS - GROUP // CHUNK + 1, CHUNKS):
            arrive(chunk)
        for at in range(rows - GROUP, rows):
            if at + lag < rows:
                push(at + lag, at + lag)
            pop(at, at)

    pl.run_scoped(contract, *[pltpu.ACC(at % 2)((2 * RANK, 256), jnp.float32) for at in range(4)])
    term_ref[...] = jnp.zeros_like(term_ref)
    term_ref[:, :, 0:RANK] = jnp.sum(sums_ref[...].reshape(8, 8, RANK, wide), axis=3)


def gradient_kernel(packed_ref, first_ref, terms_ref, gradient_ref):
    packed = packed_ref[...]
    is_third = iota(packed.shape, 0) % 3 == 2

    def gram(block):
        parts = jnp.concatenate(split(block), axis=1)
        whole = lax.dot_general(parts, parts, (((0,), (0,)), ((), ())), preferred_element_type=jnp.float32)
        wide = block.shape[1]
        whole = whole[0:wide] + whole[wide : 2 * wide]
        whole = whole[:, 0:wide] + whole[:, wide : 2 * wide]
        spans = [slice(at, at + RANK) for at in range(0, wide, RANK)]
        return sum(whole[span, span] for span in spans)

    both = gram(jnp.where(is_third, 0.0, packed)) * gram(jnp.where(is_third, packed, 0.0))
    product = jnp.sum(terms_ref[:, :, 0:RANK], axis=0)
    gradient_ref[...] = jnp.dot(first_ref[...], both, precision=HIGHEST) - product


def inhbm(value):
    return pltpu.with_memory_space_constraint(value, pltpu.HBM)


VMEM = pl.BlockSpec(memory_space=pltpu.VMEM)


def on_device(tensor, first, second, third):
    rows, js, ks = tensor.shape
    tensor = inhbm(tensor)
    own, held = pl.pallas_call(
        own_kernel,
        out_shape=(jax.ShapeDtypeStruct((128, 1, 384), jnp.float32), jax.ShapeDtypeStruct(tensor.shape, jnp.float32)),
        in_specs=[pl.BlockSpec(memory_space=pltpu.HBM)] * 3,
        out_specs=(VMEM, VMEM),
        scratch_shapes=[pltpu.VMEM((8, RANK), jnp.float32), pltpu.VMEM((4, RANK), jnp.float32), pltpu.SemaphoreType.DMA((2 + CHUNKS,))],
        compiler_params=pltpu.CompilerParams(vmem_limit_bytes=24 * 1024 * 1024),
        name="own",
    )(inhbm(second), inhbm(third), tensor)
    packed = lax.all_to_all(own, EVERY, 0, 0, tiled=True).reshape(384, 128)
    term, _ = pl.pallas_call(
        term_kernel,
        out_shape=(jax.ShapeDtypeStruct((8, 8, 4 * RANK), jnp.float32), jax.ShapeDtypeStruct(tensor.shape, jnp.float32)),
        in_specs=[pl.BlockSpec(memory_space=pltpu.HBM), VMEM, VMEM],
        out_specs=(VMEM, VMEM),
        input_output_aliases={2: 1},
        scratch_shapes=[
            pltpu.VMEM((ks, 4 * RANK), jnp.float32),
            pltpu.VMEM((js, 4 * RANK), jnp.float32),
            pltpu.VMEM((2 * RANK, ks), jnp.float32),
            pltpu.VMEM((rows, RANK, 4 * RANK), jnp.float32),
            pltpu.SemaphoreType.DMA((CHUNKS,)),
        ],
        compiler_params=pltpu.CompilerParams(vmem_limit_bytes=24 * 1024 * 1024),
        cost_estimate=pl.CostEstimate(flops=2 * rows * js * ks * 512, bytes_accessed=rows * js * ks * 4, transcendentals=0),
        name="term",
    )(tensor, packed, held)
    terms = lax.all_to_all(term, ("ja", "ka"), 0, 0, tiled=True)
    return pl.pallas_call(
        gradient_kernel,
        out_shape=jax.ShapeDtypeStruct(first.shape, jnp.float32),
        in_specs=[VMEM] * 3,
        out_specs=VMEM,
        compiler_params=pltpu.CompilerParams(vmem_limit_bytes=8 * 1024 * 1024),
        name="gradient",
    )(packed, first, terms)


def solution(mesh):
    return jax.shard_map(
        on_device,
        mesh=mesh,
        in_specs=(
            P("ia", "ja", "ka"),
            P(("ia", "ja", "ka"), None),
            P(("ja", "ia", "ka"), None),
            P(("ka", "ia", "ja"), None),
        ),
        out_specs=P(("ia", "ja", "ka"), None),
        check_vma=False,
    )
```
